768 devices in a mesh: blk: 12 (over z_hi, x), team: 64 (over z_lo, y, core).
Axes of the slice: x: 4, y: 8, z: 12 (z_hi: 3, z_lo: 4; z = z_hi * 4 + z_lo), core: 2. Of those that a mesh axis runs over, the one named last changes fastest.
Arguments:
- features: bfloat16 [98304, 256], P(('blk', 'team')), may hold values from -6 to 6
- weight: bfloat16 [256, 256], replicated, may hold values from -0.375 to 0.375
- tile_values: bfloat16 [12, 64, 12, 6, 128, 128], P('blk', 'team'), may hold values from -0.046875 to 0.046875
- tile_rows: int32 [12, 64, 12, 6], P('blk', 'team'), may hold values from 0 to 15, as said below
- tile_counts: int32 [12, 64, 12], P('blk', 'team'), may hold values from 0 to 6, as said below
- grad_out: bfloat16 [24576, 256], P(('blk', 'team')), may hold values from -6 to 6
Outputs:
- layer_out: bfloat16 [24576, 256], P(('blk', 'team'))
- grad_features: bfloat16 [98304, 256], P(('blk', 'team'))
- grad_weight: float32 [256, 256], replicated
The draws below stay inside these ranges and needn't reach their ends.
Inputs may be any that keep to these rules, and one draw needn't show every extreme that they name: `tile_rows`: within one owner's slots for one column block the row tiles are distinct. The first tile_counts[b, u, c] slots of tile_values[b, u, c] are live, the others are not part of A; some owner has 6 for some column block.
All inputs are finite; a program needn't handle non-finite values.
Results may differ from the reference program's by a relative error of at most 0.0075.
Values may be sent and summed in bfloat16 or wider, within the bound.
A program may use at most 32 MiB of HBM per device.

```python
import jax
import jax.numpy as jnp
from jax import lax

F = 256
TILE = 128
SLOTS = 6
RT = 16
TARGETS = 24576
NODES = 98304
N_BLK = 12
N_TEAM = 64


def draw_tile_rows(key, part):
    key = jax.random.fold_in(key, 11)
    scores = jax.random.randint(key, (N_BLK, N_TEAM, N_BLK, RT), 0, 2 ** 20) * RT + jnp.arange(RT, dtype=jnp.int32)
    order = jnp.argsort(scores, axis=-1, stable=True)
    return order[..., :SLOTS].astype(jnp.int32)


def draw_tile_counts(key, part):
    key = jax.random.fold_in(key, 23)
    first, second, third = jax.random.split(key, 3)
    level = jax.random.randint(first, (N_BLK, N_TEAM, 1), 1, SLOTS + 1)
    base = jax.random.randint(second, (N_BLK, N_TEAM, N_BLK), 0, SLOTS + 1)
    counts = jnp.minimum(base, level).reshape(-1)
    spot = jax.random.randint(third, (), 0, N_BLK * N_TEAM * N_BLK)
    filled = jnp.where(jnp.arange(N_BLK * N_TEAM * N_BLK) == spot, SLOTS, counts)
    return filled.reshape(N_BLK, N_TEAM, N_BLK).astype(jnp.int32)


def block_scale(key, dims, pieces, least, largest):
    level = 1.0
    for position, blocks in pieces:
        steps = jax.random.uniform(jax.random.fold_in(jax.random.fold_in(key, 6), position), (blocks,), jnp.float32, least / len(pieces), largest / len(pieces))
        level = level * jnp.repeat(jnp.exp(steps), dims[position] // blocks).reshape((-1,) + (1,) * (len(dims) - 1 - position))
    return level


def gaussian(key, shape, width, most, cuts=(), kind=jnp.bfloat16):
    values = jax.random.normal(key, shape, jnp.float32) * width
    if len(cuts) > 0:
        values = block_scale(key, shape, cuts, -0.22, 0.18) * values
    return jnp.clip(values, min=-most, max=most).astype(kind)


def setup_inputs(seed: int = 0) -> dict:
    key_of = jax.random.split(jax.random.key(seed), 7)
    features = gaussian(key_of[0], (NODES, F), 1.0, 6.0, ((0, 768),))
    weight = gaussian(key_of[1], (F, F), F ** -0.5, 0.375)
    tile_values = gaussian(key_of[2], (N_BLK, N_TEAM, N_BLK, SLOTS, TILE, TILE), (N_TEAM * N_BLK * TILE * SLOTS // (2 * RT)) ** -0.5, 0.046875, ((0, 12), (1, 64)))
    tile_rows = draw_tile_rows(jax.random.fold_in(key_of[6], 71), 0)
    tile_counts = draw_tile_counts(jax.random.fold_in(key_of[6], 71), 0)
    grad_out = gaussian(key_of[5], (TARGETS, F), 1.0, 6.0, ((0, 768),))
    return dict(features=features, weight=weight, tile_values=tile_values, tile_rows=tile_rows, tile_counts=tile_counts, grad_out=grad_out)


def reference(features, weight, tile_values, tile_rows, tile_counts, grad_out):
    hidden = jnp.dot(features, weight, preferred_element_type=jnp.float32).astype(jnp.bfloat16)
    hid = hidden.astype(jnp.float32).reshape(N_BLK, N_TEAM, TILE, F)
    live = jnp.arange(SLOTS, dtype=jnp.int32)[None, None, None, :] < tile_counts[..., None]
    onehot = ((tile_rows[..., None] == jnp.arange(RT, dtype=jnp.int32)) & live[..., None]).astype(jnp.float32)

    def forward_block(index):
        tiles = tile_values[index].astype(jnp.float32)
        prod = jnp.einsum("uckij,cujf->uckif", tiles, hid, precision=lax.Precision.HIGHEST)
        return jnp.einsum("uckr,uckif->rif", onehot[index], prod, precision=lax.Precision.HIGHEST)

    pre = lax.map(forward_block, jnp.arange(N_BLK, dtype=jnp.int32)).reshape(TARGETS, F)
    sig = jax.nn.sigmoid(pre)
    layer_out = (pre * sig).astype(jnp.bfloat16)
    grad_pre = (grad_out.astype(jnp.float32) * sig * (1.0 + pre * (1.0 - sig))).astype(jnp.bfloat16)
    grads = grad_pre.astype(jnp.float32).reshape(N_BLK, RT, TILE, F)

    def backward_block(carry, index):
        tiles = tile_values[index].astype(jnp.float32)
        chosen = jnp.einsum("uckr,rif->uckif", onehot[index], grads[index], precision=lax.Precision.HIGHEST)
        return carry + jnp.einsum("uckij,uckif->cujf", tiles, chosen, precision=lax.Precision.HIGHEST), None

    start = jnp.zeros((N_BLK, N_TEAM, TILE, F), jnp.float32)
    grad_hidden, _ = lax.scan(backward_block, start, jnp.arange(N_BLK, dtype=jnp.int32))
    grad_hidden = grad_hidden.reshape(NODES, F).astype(jnp.bfloat16)
    grad_features = jnp.dot(grad_hidden, weight.T, preferred_element_type=jnp.float32).astype(jnp.bfloat16)
    grad_weight = jnp.dot(features.T, grad_hidden, preferred_element_type=jnp.float32)
    return layer_out, grad_features, grad_weight
```

```python
import functools

import jax
import jax.numpy as jnp
from jax import lax
from jax.experimental import pallas as pl
from jax.experimental.pallas import tpu as pltpu
from jax.sharding import PartitionSpec as P

MESH = pl.DeviceIdType.MESH
BF = jnp.bfloat16
F32 = jnp.float32
ZH, NX, ZL, NY = 3, 4, 4, 8
NC = ZH * NX
SLOTS, RT, TILE, HALF, OWN = 6, 16, 128, 128, 32
NTILES = NC * SLOTS
N_COPIES = 160


def kernel(
    feat, weight, tiles, rows, counts, gout,
    out, gfeat, gweight,
    tb, tT, inv, ridx, xs, acc, pc, rc, s, ry0, rz0, rz1, ry1, t0, t1, gg0, gg1,
    part, fa, fb, fc, ff, fs, fz, gw1s, gw1, gw2s, gw2, gw3, gw4, gw5, gwa,
    tile_sem, send_sem, recv_sem,
):
    blk, team = lax.axis_index("blk"), lax.axis_index("team")
    zh, x = blk // NX, blk % NX
    zl, y, co = team // (2 * NY), (team // 2) % NY, team % 2

    def at(zh_=zh, x_=x, zl_=zl, y_=y, co_=co):
        return (zh_ * NX + x_, (zl_ * NY + y_) * 2 + co_)

    def off(value, d, size):
        return (value + d + size) % size

    started = []

    def send(src, dst, device):
        i = len(started)
        copy = pltpu.make_async_remote_copy(
            src_ref=src, dst_ref=dst, send_sem=send_sem.at[i], recv_sem=recv_sem.at[i],
            device_id=device, device_id_type=MESH,
        )
        copy.start()
        started.append(copy)
        return copy

    barrier = pltpu.get_barrier_semaphore()
    partners = [at(co_=1 - co)]
    partners += [at(y_=off(y, d, NY)) for d in range(1, NY)]
    partners += [at(zl_=off(zl, d, ZL)) for d in range(1, ZL)]
    partners += [at(x_=off(x, d, NX)) for d in range(1, NX)]
    partners += [at(zh_=off(zh, d, ZH)) for d in range(1, ZH)]
    for device in partners:
        pl.semaphore_signal(barrier, inc=1, device_id=device, device_id_type=MESH)
    load = pltpu.make_async_copy(tiles, tb.at[pl.ds(0, NTILES)], tile_sem)
    load.start()
    for h in range(2):
        xs[h, blk] = feat[:, h * HALF:(h + 1) * HALF]
    tb[NTILES] = jnp.zeros((TILE, TILE), BF)
    for ref in (gg0, gg1):
        ref[ZL] = jnp.zeros((NY, 2, OWN, HALF), BF)

    def index_body(c, carry):
        count = counts[0, 0, c]
        rowof = [jnp.where(k < count, rows[0, 0, c, k], RT) for k in range(SLOTS)]
        for k in range(SLOTS):
            ridx[c * SLOTS + k] = rowof[k]
        for r in range(RT):
            found = NTILES
            for k in range(SLOTS):
                found = jnp.where(rowof[k] == r, c * SLOTS + k, found)
            inv[c * RT + r] = found
        return carry

    lax.fori_loop(0, NC, index_body, 0)
    pl.semaphore_wait(barrier, len(partners))

    own_z, own_x = [], []
    sign = (1, -1)
    for h in range(2):
        block = xs.at[h, blk]
        own_z.append([send(block, block, at(zh_=off(zh, d, ZH))) for d in range(1, ZH)])
        own_x.append([send(block, block, at(x_=off(x, sign[h], NX))), send(block, block, at(x_=off(x, -sign[h], NX)))])

    def slot(dz, dx):
        return off(zh, dz, ZH) * NX + off(x, dx, NX)

    def forward_group(h, dz, first):
        cols = [slot(dz, dx) for dx in range(NX)]
        right = jnp.concatenate([xs[h, c] for c in cols], axis=0)

        def step(r, carry):
            left = jnp.concatenate([tb[inv[c * RT + r]] for c in cols], axis=1)
            prod = jnp.dot(left, right, preferred_element_type=F32).reshape(2, 2, OWN, HALF)
            zt, yt = r // (NY // 2), (r % (NY // 2)) * 2
            if first:
                acc[h, zt, pl.ds(yt, 2)] = prod
            else:
                acc[h, zt, pl.ds(yt, 2)] += prod
            return carry

        lax.fori_loop(0, RT, step, 0, unroll=2)

    def pass_on(h, dz):
        block = xs.at[h, slot(dz, -sign[h])]
        return send(block, block, at(x_=off(x, sign[h], NX)))

    far = [[None] * ZH, [None] * ZH]
    near = [[None] * ZH, [None] * ZH]
    load.wait()
    for h in range(2):
        own_x[h][0].wait_recv()
        far[h][0] = pass_on(h, 0)

    def spread(h):
        for d in range(1, ZH):
            own_z[h][d - 1].wait_recv()
            block = xs.at[h, slot(-d, 0)]
            near[h][ZH - d] = [
                send(block, block, at(x_=off(x, sign[h], NX))),
                send(block, block, at(x_=off(x, -sign[h], NX))),
            ]

    def group_zero(h):
        own_x[h][1].wait_recv()
        far[h][0].wait_recv()
        forward_group(h, 0, True)

    def relay(h):
        for d in range(1, ZH):
            near[h][ZH - d][0].wait_recv()
            far[h][ZH - d] = pass_on(h, ZH - d)

    def group_rest(h):
        for d in range(1, ZH):
            near[h][ZH - d][1].wait_recv()
            far[h][ZH - d].wait_recv()
            forward_group(h, ZH - d, False)

    def to_partner_core(h):
        pc[h] = acc[h, :, :, 1 - co].astype(BF)
        return send(pc.at[h], rc.at[h], at(co_=1 - co))

    def add_partner_core(h, copy):
        copy.wait_recv()
        s[h] = (acc[h, :, :, co] + rc[h].astype(F32)).astype(BF)

    def transpose_body(c, carry):
        for k in range(SLOTS):
            tT[c, :, k * TILE:(k + 1) * TILE] = tb[c * SLOTS + k].T
        return carry

    spread(0)
    group_zero(0)
    relay(0)
    spread(1)
    group_rest(0)
    core0 = to_partner_core(0)
    relay(1)
    group_zero(1)
    add_partner_core(0, core0)
    y0 = [send(s.at[0, :, off(y, d, NY)], ry0.at[d], at(y_=off(y, d, NY))) for d in range(1, NY)]
    group_rest(1)
    core1 = to_partner_core(1)
    lax.fori_loop(0, NC // 2, transpose_body, 0)
    add_partner_core(1, core1)
    z1 = [send(s.at[1, off(zl, d, ZL)], rz1.at[d], at(zl_=off(zl, d, ZL))) for d in range(1, ZL)]
    lax.fori_loop(NC // 2, NC, transpose_body, 0)

    total = s[0, :, y].astype(F32)
    for d in range(1, NY):
        y0[d - 1].wait_recv()
        total += ry0[d].astype(F32)
    t0[...] = total.astype(BF)
    z0 = [send(t0.at[off(zl, d, ZL)], rz0.at[d], at(zl_=off(zl, d, ZL))) for d in range(1, ZL)]
    total = s[1, zl].astype(F32)
    for d in range(1, ZL):
        z1[d - 1].wait_recv()
        total += rz1[d].astype(F32)
    t1[...] = total.astype(BF)
    y1 = [send(t1.at[off(y, d, NY)], ry1.at[d], at(y_=off(y, d, NY))) for d in range(1, NY)]
    ax0 = t0[zl].astype(F32)
    for d in range(1, ZL):
        z0[d - 1].wait_recv()
        ax0 += rz0[d].astype(F32)
    ax1 = t1[y].astype(F32)
    for d in range(1, NY):
        y1[d - 1].wait_recv()
        ax1 += ry1[d].astype(F32)

    ax = jnp.concatenate([ax0, ax1], axis=1)
    high = ax.astype(BF)
    low = (ax - high.astype(F32)).astype(BF)
    w = weight[...]
    pre = jnp.dot(high, w, preferred_element_type=F32) + jnp.dot(low, w, preferred_element_type=F32)
    sig = jax.nn.sigmoid(pre)
    out[...] = (pre * sig).astype(BF)
    grad = (gout[...].astype(F32) * sig * (1.0 + pre * (1.0 - sig))).astype(BF)
    back = lax.dot_general(grad, w, (((1,), (1,)), ((), ())), preferred_element_type=F32).astype(BF)
    gg0[zl, y, co] = back[:, :HALF]
    gg1[zl, y, co] = back[:, HALF:]

    mine0, mine1 = gg0.at[zl, y, co], gg1.at[zl, y, co]
    a0 = [send(mine0, mine0, at(zl_=off(zl, d, ZL))) for d in range(1, ZL)]
    a1 = [send(mine1, mine1, at(y_=off(y, d, NY))) for d in range(1, NY)]

    gw = lax.dot_general(
        jnp.concatenate([high, low], axis=0), jnp.concatenate([grad, grad], axis=0),
        (((0,), (0,)), ((), ())), preferred_element_type=F32,
    ).reshape(2, TILE, 2 * HALF)
    gw1s[...] = gw
    g1 = send(gw1s.at[1 - co], gw1, at(co_=1 - co))

    other = at(co_=1 - co)
    for copy in a0:
        copy.wait_recv()
    line = gg0.at[pl.ds(0, ZL), y, co]
    b0 = [send(line, line, at(y_=off(y, d, NY))) for d in range(1, NY)]
    c0 = [send(line, line, other)]
    for copy in a1:
        copy.wait_recv()
    line = gg1.at[zl, :, co]
    b1 = [send(line, line, at(zl_=off(zl, d, ZL))) for d in range(1, ZL)]
    c1 = [send(line, line, other)]
    g1.wait_recv()
    gw2s[...] = (gw1s[co] + gw1[...]).reshape(NY, OWN // 2, 2 * HALF).astype(BF)
    g2 = [send(gw2s.at[off(y, d, NY)], gw2.at[d], at(y_=off(y, d, NY))) for d in range(1, NY)]
    for d in range(1, NY):
        b0[d - 1].wait_recv()
        line = gg0.at[pl.ds(0, ZL), off(y, -d, NY), co]
        c0.append(send(line, line, other))
    for d in range(1, ZL):
        b1[d - 1].wait_recv()
        line = gg1.at[off(zl, -d, ZL), :, co]
        c1.append(send(line, line, other))
    sub = gw2s[y].astype(F32)
    for d in range(1, NY):
        g2[d - 1].wait_recv()
        sub += gw2[d].astype(F32)
    gw3[x] = sub
    g3 = [send(gw3.at[x], gw3.at[x], at(x_=off(x, d, NX))) for d in range(1, NX)]

    def back_term(h, dz, dx):
        ref = (gg0, gg1)[h]
        c = slot(dz, dx)
        picks = []
        for k in range(SLOTS):
            r = ridx[c * SLOTS + k]
            picks.append(ref[r >> 2, pl.ds((r & 3) * 2, 2)].reshape(TILE, HALF))
        return jnp.dot(tT[c], jnp.concatenate(picks, axis=0), preferred_element_type=F32)

    order = (1, 2, 0)

    def first_products(h):
        ahead, behind = at(x_=off(x, sign[h], NX)), at(x_=off(x, -sign[h], NX))
        sa, sb = {}, {}
        for dz in order:
            part[h, 0, dz] = back_term(h, dz, 2).astype(BF)
            sa[dz] = send(part.at[h, 0, dz], fa.at[h, dz], ahead)
            part[h, 1, dz] = back_term(h, dz, -sign[h]).astype(BF)
            sb[dz] = send(part.at[h, 1, dz], fb.at[h, dz], behind)
        return sa, sb

    def second_products(h, sa):
        ahead = at(x_=off(x, sign[h], NX))
        sc = {}
        for dz in order:
            term = back_term(h, dz, sign[h])
            sa[dz].wait_recv()
            ff[h, dz] = (term + fa[h, dz].astype(F32)).astype(BF)
            sc[dz] = send(ff.at[h, dz], fc.at[h, dz], ahead)
        return sc

    def last_products(h, sb, sc):
        sz = []
        for dz in order:
            term = back_term(h, dz, 0)
            sb[dz].wait_recv()
            term += fb[h, dz].astype(F32)
            sc[dz].wait_recv()
            term += fc[h, dz].astype(F32)
            if dz:
                fs[h, dz - 1] = term.astype(BF)
                sz.append(send(fs.at[h, dz - 1], fz.at[h, dz - 1], at(zh_=off(zh, dz, ZH))))
        return sz, term

    def finish(h, sz, term):
        for dz in range(1, ZH):
            sz[dz - 1].wait_recv()
            term += fz[h, dz - 1].astype(F32)
        gfeat[:, h * HALF:(h + 1) * HALF] = term.astype(BF)

    for copy in c0:
        copy.wait_recv()
    sa0, sb0 = first_products(0)
    for copy in c1:
        copy.wait_recv()
    sa1, sb1 = first_products(1)
    sc0 = second_products(0, sa0)
    for copy in g3:
        copy.wait_recv()
    gw4[zl] = (gw3[0] + gw3[1]) + (gw3[2] + gw3[3])
    g4 = [send(gw4.at[zl], gw4.at[zl], at(zl_=off(zl, d, ZL))) for d in range(1, ZL)]
    sc1 = second_products(1, sa1)
    sz0, term0 = last_products(0, sb0, sc0)
    for copy in g4:
        copy.wait_recv()
    gw5[zh] = (gw4[0] + gw4[1]) + (gw4[2] + gw4[3])
    g5 = [send(gw5.at[zh], gw5.at[zh], at(zh_=off(zh, d, ZH))) for d in range(1, ZH)]
    sz1, term1 = last_products(1, sb1, sc1)
    for copy in g5:
        copy.wait_recv()
    gwa[co, y] = gw5[0] + gw5[1] + gw5[2]
    g6 = [send(gwa.at[co, y], gwa.at[co, y], at(y_=off(y, d, NY))) for d in range(1, NY)]
    finish(0, sz0, term0)
    for copy in g6:
        copy.wait_recv()
    g7 = send(gwa.at[co], gwa.at[co], other)
    finish(1, sz1, term1)
    g7.wait_recv()
    gweight[...] = gwa[...].reshape(2 * HALF, 2 * HALF)
    for copy in started:
        copy.wait_send()


def body(features, weight, tile_values, tile_rows, tile_counts, grad_out):
    vmem = pl.BlockSpec(memory_space=pltpu.VMEM)
    smem = pl.BlockSpec(memory_space=pltpu.SMEM)
    rows16 = OWN // 2
    return pl.pallas_call(
        kernel,
        out_shape=(
            jax.ShapeDtypeStruct(grad_out.shape, BF),
            jax.ShapeDtypeStruct(features.shape, BF),
            jax.ShapeDtypeStruct(weight.shape, F32),
        ),
        in_specs=[vmem, vmem, pl.BlockSpec(memory_space=pl.ANY), smem, smem, vmem],
        out_specs=(vmem, vmem, vmem),
        scratch_shapes=[
            pltpu.VMEM((NTILES + 1, TILE, TILE), BF),
            pltpu.VMEM((NC, TILE, SLOTS * TILE), BF),
            pltpu.SMEM((NC * RT,), jnp.int32),
            pltpu.SMEM((NTILES,), jnp.int32),
            pltpu.VMEM((2, NC, TILE, HALF), BF),
            pltpu.VMEM((2, ZL, NY, 2, OWN, HALF), F32),
            pltpu.VMEM((2, ZL, NY, OWN, HALF), BF),
            pltpu.VMEM((2, ZL, NY, OWN, HALF), BF),
            pltpu.VMEM((2, ZL, NY, OWN, HALF), BF),
            pltpu.VMEM((NY, ZL, OWN, HALF), BF),
            pltpu.VMEM((ZL, OWN, HALF), BF),
            pltpu.VMEM((ZL, NY, OWN, HALF), BF),
            pltpu.VMEM((NY, OWN, HALF), BF),
            pltpu.VMEM((ZL, OWN, HALF), BF),
            pltpu.VMEM((NY, OWN, HALF), BF),
            pltpu.VMEM((ZL + 1, NY, 2, OWN, HALF), BF),
            pltpu.VMEM((ZL + 1, NY, 2, OWN, HALF), BF),
            pltpu.VMEM((2, 2, ZH, TILE, HALF), BF),
            pltpu.VMEM((2, ZH, TILE, HALF), BF),
            pltpu.VMEM((2, ZH, TILE, HALF), BF),
            pltpu.VMEM((2, ZH, TILE, HALF), BF),
            pltpu.VMEM((2, ZH, TILE, HALF), BF),
            pltpu.VMEM((2, ZH - 1, TILE, HALF), BF),
            pltpu.VMEM((2, ZH - 1, TILE, HALF), BF),
            pltpu.VMEM((2, TILE, 2 * HALF), F32),
            pltpu.VMEM((TILE, 2 * HALF), F32),
            pltpu.VMEM((NY, rows16, 2 * HALF), BF),
            pltpu.VMEM((NY, rows16, 2 * HALF), BF),
            pltpu.VMEM((NX, rows16, 2 * HALF), F32),
            pltpu.VMEM((ZL, rows16, 2 * HALF), F32),
            pltpu.VMEM((ZH, rows16, 2 * HALF), F32),
            pltpu.VMEM((2, NY, rows16, 2 * HALF), F32),
            pltpu.SemaphoreType.DMA,
            pltpu.SemaphoreType.DMA((N_COPIES,)),
            pltpu.SemaphoreType.DMA((N_COPIES,)),
        ],
        compiler_params=pltpu.CompilerParams(
            collective_id=0, has_side_effects=True, vmem_limit_bytes=40 * 2 ** 20
        ),
    )(features, weight, tile_values.reshape(NTILES, TILE, TILE), tile_rows, tile_counts, grad_out)


def solution(mesh):
    in_specs = (
        P(("blk", "team"), None),
        P(),
        P("blk", "team", None, None, None, None),
        P("blk", "team", None, None),
        P("blk", "team", None),
        P(("blk", "team"), None),
    )
    out_specs = (P(("blk", "team"), None), P(("blk", "team"), None), P())
    return jax.shard_map(body, mesh=mesh, in_specs=in_specs, out_specs=out_specs, check_vma=False)
```

```python
import math

import jax
import jax.numpy as jnp
from jax import lax
from jax.experimental import pallas as pl
from jax.experimental.pallas import tpu as pltpu
from jax.sharding import PartitionSpec as P

MESH = pl.DeviceIdType.MESH
BF = jnp.bfloat16
F32 = jnp.float32
ZH, NX, ZL, NY = 3, 4, 4, 8
NC = ZH * NX
SLOTS, RT, TILE, HALF, OWN = 6, 16, 128, 128, 32
NTILES = NC * SLOTS
N_GROUPS, N_UNITS = 47, 320


def kernel(
    feat, weight, tiles, rows_in, counts_in, gout_in,
    out, gfeat, gweight,
    tb, tT, wv, gout, rows, counts, inv_v, ridx_v, inv, ridx, xs, acc, pc, rc, s, ry0, rz0, rz1, ry1, t0, t1, gg0, gg1,
    part, fx, own, fs, fz, gw1s, gw1, gw2s, gw2, gw3, gw4, gw5, gwa,
    spare, load_sem, send_sem, recv_sem,
):
    blk, team = lax.axis_index("blk"), lax.axis_index("team")
    zh, x = blk // NX, blk % NX
    zl, y, co = team // (2 * NY), (team // 2) % NY, team % 2

    def at(zh_=zh, x_=x, zl_=zl, y_=y, co_=co):
        return (zh_ * NX + x_, (zl_ * NY + y_) * 2 + co_)

    def off(value, d, size):
        return (value + d + size) % size

    other = at(co_=1 - co)
    x_peers = [at(x_=off(x, d, NX)) for d in range(1, NX)]
    y_peers = [at(y_=off(y, d, NY)) for d in range(1, NY)]
    zl_peers = [at(zl_=off(zl, d, ZL)) for d in range(1, ZL)]
    zh_peers = [at(zh_=off(zh, d, ZH)) for d in range(1, ZH)]

    barrier = pltpu.get_barrier_semaphore()
    partners = zh_peers + y_peers + x_peers + zl_peers + [other]
    for device in partners:
        pl.semaphore_signal(barrier, inc=1, device_id=device, device_id_type=MESH)

    loads = []

    def load(src, dst):
        copy = pltpu.make_async_copy(src, dst, load_sem.at[len(loads)])
        copy.start()
        loads.append(copy)
        return copy

    load_x = [load(feat.at[:, h * HALF:(h + 1) * HALF], xs.at[h, blk]) for h in range(2)]
    load_index = [load(rows_in, rows), load(counts_in, counts)]
    load_tiles = load(tiles, tb.at[pl.ds(0, NTILES)])
    load_rest = [load(weight, wv), load(gout_in, gout)]

    unit = OWN * HALF * 2
    groups, sent = [], [0, 0]

    def remote(src, dst, group, phase, device):
        return pltpu.make_async_remote_copy(
            src_ref=src, dst_ref=dst, send_sem=send_sem.at[phase], recv_sem=recv_sem.at[group],
            device_id=device, device_id_type=MESH,
        )

    def size(ref):
        return math.prod(ref.shape) * ref.dtype.itemsize // unit

    class Group:
        def __init__(self, phase):
            self.index, self.phase, self.units = len(groups), phase, 0
            groups.append(self)

        def count(self, units):
            self.units += units
            sent[self.phase] += units

        def send(self, src, dst, device):
            remote(src, dst, self.index, self.phase, device).start()
            self.count(size(src))

        def wait(self):
            ref = spare.at[pl.ds(0, self.units)]
            remote(ref, ref, self.index, self.phase, other).wait_recv()

    def send_all(phase, sources, targets, devices):
        group = Group(phase)
        for src, dst, device in zip(sources, targets, devices):
            group.send(src, dst, device)
        return group

    def send_same(phase, ref, devices):
        return send_all(phase, [ref] * len(devices), [ref] * len(devices), devices)

    for copy in load_x:
        copy.wait()
    pl.semaphore_wait(barrier, len(partners))

    own_z = [[send_same(0, xs.at[h, blk], [device]) for device in zh_peers] for h in range(2)]
    own_x = [send_same(0, xs.at[h, blk], x_peers) for h in range(2)]

    tb[NTILES] = jnp.zeros((TILE, TILE), BF)
    for ref in (gg0, gg1):
        ref[ZL] = jnp.zeros((NY, 2, OWN, HALF), BF)

    for copy in load_index:
        copy.wait()
    live = counts[...]
    first_tile = lax.broadcasted_iota(jnp.int32, (1, NC), 1) * SLOTS
    rowof = [jnp.where(k < live, rows[k], RT) for k in range(SLOTS)]
    for k in range(SLOTS):
        ridx_v[k] = rowof[k]
    for r in range(RT):
        found = jnp.full((1, NC), NTILES, jnp.int32)
        for k in range(SLOTS):
            found = jnp.where(rowof[k] == r, first_tile + k, found)
        inv_v[r] = found
    load_index = [load(inv_v, inv), load(ridx_v, ridx)]
    for copy in load_index:
        copy.wait()
    load_tiles.wait()

    def slot(dz, dx):
        return off(zh, dz, ZH) * NX + off(x, dx, NX)

    def forward_group(h, dz, first, last):
        cols = [slot(dz, dx) for dx in range(NX)]
        right = jnp.concatenate([xs[h, c] for c in cols], axis=0)

        def step(r, carry):
            left = jnp.concatenate([tb[inv[r, 0, c]] for c in cols], axis=1)
            prod = jnp.dot(left, right, preferred_element_type=F32).reshape(2, 2, OWN, HALF)
            zt, yt = r // (NY // 2), (r % (NY // 2)) * 2
            if not first:
                prod += acc[h, zt, pl.ds(yt, 2)]
            acc[h, zt, pl.ds(yt, 2)] = prod
            if last:
                pc[h, zt, pl.ds(yt, 2)] = prod.astype(BF)
            return carry

        lax.fori_loop(0, RT, step, 0, unroll=2)

    def group(h, dz, arrivals):
        arrivals.wait()
        forward_group(h, dz, dz == 0, dz == 1)

    def spread(h, d):
        own_z[h][d - 1].wait()
        return send_same(0, xs.at[h, slot(-d, 0)], x_peers)

    def to_partner_core(h):
        return send_all(0, [pc.at[h, :, :, 1 - co]], [rc.at[h]], [other])

    def add_partner_core(h, copy):
        copy.wait()
        s[h] = (acc[h, :, :, co] + rc[h].astype(F32)).astype(BF)

    def transpose_body(c, carry):
        for k in range(SLOTS):
            tT[c, :, k * TILE:(k + 1) * TILE] = tb[c * SLOTS + k].T
        return carry

    group(0, 0, own_x[0])
    near = [[None] * ZH, [None] * ZH]
    for d in range(1, ZH):
        near[0][ZH - d] = spread(0, d)
    group(1, 0, own_x[1])
    for d in range(1, ZH):
        near[1][ZH - d] = spread(1, d)
    for d in range(1, ZH):
        group(0, ZH - d, near[0][ZH - d])
    core0 = to_partner_core(0)
    for d in range(1, ZH):
        group(1, ZH - d, near[1][ZH - d])
    core1 = to_partner_core(1)
    add_partner_core(0, core0)
    y0 = send_all(0, [s.at[0, :, off(y, d, NY)] for d in range(1, NY)], [ry0.at[d] for d in range(1, NY)], y_peers)
    add_partner_core(1, core1)
    z1 = send_all(0, [s.at[1, off(zl, d, ZL)] for d in range(1, ZL)], [rz1.at[d] for d in range(1, ZL)], zl_peers)
    lax.fori_loop(0, NC, transpose_body, 0)
    for copy in load_rest:
        copy.wait()

    def add_up(total, ref):
        for d in range(1, ref.shape[0]):
            total += ref[d].astype(F32)
        return total

    z1.wait()
    t1[...] = add_up(s[1, zl].astype(F32), rz1).astype(BF)
    y1 = send_all(0, [t1.at[off(y, d, NY)] for d in range(1, NY)], [ry1.at[d] for d in range(1, NY)], y_peers)
    y0.wait()
    t0[...] = add_up(s[0, :, y].astype(F32), ry0).astype(BF)
    z0 = send_all(0, [t0.at[off(zl, d, ZL)] for d in range(1, ZL)], [rz0.at[d] for d in range(1, ZL)], zl_peers)
    y1.wait()
    ax1 = add_up(t1[y].astype(F32), ry1)
    z0.wait()
    ax0 = add_up(t0[zl].astype(F32), rz0)

    ax = jnp.concatenate([ax0, ax1], axis=1)
    high = ax.astype(BF)
    low = (ax - high.astype(F32)).astype(BF)
    w = wv[...]
    pre = jnp.dot(high, w, preferred_element_type=F32) + jnp.dot(low, w, preferred_element_type=F32)
    sig = jax.nn.sigmoid(pre)
    grad = (gout[...].astype(F32) * sig * (1.0 + pre * (1.0 - sig))).astype(BF)
    back = lax.dot_general(grad, w, (((1,), (1,)), ((), ())), preferred_element_type=F32).astype(BF)
    gg0[zl, y, co] = back[:, :HALF]
    gg1[zl, y, co] = back[:, HALF:]

    a0 = send_same(1, gg0.at[zl, y, co], zl_peers)
    a1 = send_same(1, gg1.at[zl, y, co], y_peers)
    out[...] = (pre * sig).astype(BF)

    gw1s[...] = lax.dot_general(
        jnp.concatenate([high, low], axis=0), jnp.concatenate([grad, grad], axis=0),
        (((0,), (0,)), ((), ())), preferred_element_type=F32,
    ).reshape(2, TILE, 2 * HALF)
    g1 = send_all(1, [gw1s.at[1 - co]], [gw1], [other])
    g1.wait()
    gw2s[...] = (gw1s[co] + gw1[...]).reshape(NY, OWN // 2, 2 * HALF).astype(BF)
    g2 = send_all(1, [gw2s.at[off(y, d, NY)] for d in range(1, NY)], [gw2.at[d] for d in range(1, NY)], y_peers)

    a0.wait()
    line = gg0.at[pl.ds(0, ZL), y, co]
    b0 = [send_all(1, [line], [line], [device]) for device in y_peers]
    c0 = send_same(1, line, [other])
    a1.wait()
    line = gg1.at[zl, :, co]
    b1 = [send_all(1, [line], [line], [device]) for device in zl_peers]
    c1 = send_same(1, line, [other])
    g2.wait()
    gw3[zl] = add_up(gw2s[y].astype(F32), gw2)
    g3 = send_same(1, gw3.at[zl], zl_peers)
    for d in range(1, ZL):
        b1[d - 1].wait()
        line = gg1.at[off(zl, -d, ZL), :, co]
        c1.send(line, line, other)
    g3.wait()
    gw4[x] = (gw3[0] + gw3[1]) + (gw3[2] + gw3[3])
    g4 = send_same(1, gw4.at[x], x_peers)
    for d in range(1, NY):
        b0[d - 1].wait()
        line = gg0.at[pl.ds(0, ZL), off(y, -d, NY), co]
        c0.send(line, line, other)

    def back_term(h, dz, dx):
        ref = (gg0, gg1)[h]
        c = slot(dz, dx)
        picks = []
        for k in range(SLOTS):
            r = ridx[k, 0, c]
            picks.append(ref[r >> 2, pl.ds((r & 3) * 2, 2)].reshape(TILE, HALF))
        return jnp.dot(tT[c], jnp.concatenate(picks, axis=0), preferred_element_type=F32)

    sx = {}

    def products(h, low, count):
        base = len(groups)
        for dz in range(low, low + count):
            sx[h, dz] = Group(1)
            sx[h, dz].count((NX - 1) * size(part.at[h, dz, 0]))

        def step(i, carry):
            dz, dx = low + i // (NX - 1), 1 + i % (NX - 1)
            part[h, dz, dx] = back_term(h, dz, dx).astype(BF)
            remote(part.at[h, dz, dx], fx.at[h, dz, dx], base + i // (NX - 1), 1, at(x_=off(x, dx, NX))).start()
            return carry

        lax.fori_loop(0, count * (NX - 1), step, 0)

    def own_products(h):
        def step(dz, carry):
            own[h, dz] = back_term(h, dz, 0)
            return carry

        lax.fori_loop(0, ZH, step, 0)

    def total_over_x(h, dz):
        sx[h, dz].wait()
        return add_up(own[h, dz], fx.at[h, dz])

    sz = {}

    def to_z(h, dz):
        fs[h, dz - 1] = total_over_x(h, dz).astype(BF)
        sz[h, dz] = send_all(1, [fs.at[h, dz - 1]], [fz.at[h, dz - 1]], [zh_peers[dz - 1]])

    def finish(h):
        term = own[h, 0]
        for dz in range(1, ZH):
            sz[h, dz].wait()
            term += fz[h, dz - 1].astype(F32)
        gfeat[:, h * HALF:(h + 1) * HALF] = term.astype(BF)

    c1.wait()
    products(1, 1, 2)
    g4.wait()
    gw5[zh] = (gw4[0] + gw4[1]) + (gw4[2] + gw4[3])
    g5 = send_same(1, gw5.at[zh], zh_peers)
    c0.wait()
    products(0, 1, 2)
    own_products(1)
    for dz in range(1, ZH):
        to_z(1, dz)
    own_products(0)
    for dz in range(1, ZH):
        to_z(0, dz)
    products(1, 0, 1)
    products(0, 0, 1)
    g5.wait()
    gwa[co, y] = (gw5[0] + gw5[1] + gw5[2]).astype(BF)
    g6 = send_same(1, gwa.at[co, y], y_peers)
    for h in (1, 0):
        own[h, 0] = total_over_x(h, 0)
    finish(1)
    g6.wait()
    g7 = send_same(1, gwa.at[co], [other])
    finish(0)
    g7.wait()
    gweight[...] = gwa[...].reshape(2 * HALF, 2 * HALF).astype(F32)
    for phase in range(2):
        ref = spare.at[pl.ds(0, sent[phase])]
        remote(ref, ref, 0, phase, other).wait_send()


def body(features, weight, tile_values, tile_rows, tile_counts, grad_out):
    vmem = pl.BlockSpec(memory_space=pltpu.VMEM)
    hbm = pl.BlockSpec(memory_space=pltpu.HBM)
    rows16 = OWN // 2
    return pl.pallas_call(
        kernel,
        out_shape=(
            jax.ShapeDtypeStruct(grad_out.shape, BF),
            jax.ShapeDtypeStruct(features.shape, BF),
            jax.ShapeDtypeStruct(weight.shape, F32),
        ),
        in_specs=[hbm] * 6,
        out_specs=(vmem, vmem, vmem),
        scratch_shapes=[
            pltpu.VMEM((NTILES + 1, TILE, TILE), BF),
            pltpu.VMEM((NC, TILE, SLOTS * TILE), BF),
            pltpu.VMEM(weight.shape, BF),
            pltpu.VMEM(grad_out.shape, BF),
            pltpu.VMEM((SLOTS, 1, NC), jnp.int32),
            pltpu.VMEM((1, NC), jnp.int32),
            pltpu.VMEM((RT, 1, NC), jnp.int32),
            pltpu.VMEM((SLOTS, 1, NC), jnp.int32),
            pltpu.SMEM((RT, 1, NC), jnp.int32),
            pltpu.SMEM((SLOTS, 1, NC), jnp.int32),
            pltpu.VMEM((2, NC, TILE, HALF), BF),
            pltpu.VMEM((2, ZL, NY, 2, OWN, HALF), F32),
            pltpu.VMEM((2, ZL, NY, 2, OWN, HALF), BF),
            pltpu.VMEM((2, ZL, NY, OWN, HALF), BF),
            pltpu.VMEM((2, ZL, NY, OWN, HALF), BF),
            pltpu.VMEM((NY, ZL, OWN, HALF), BF),
            pltpu.VMEM((ZL, OWN, HALF), BF),
            pltpu.VMEM((ZL, NY, OWN, HALF), BF),
            pltpu.VMEM((NY, OWN, HALF), BF),
            pltpu.VMEM((ZL, OWN, HALF), BF),
            pltpu.VMEM((NY, OWN, HALF), BF),
            pltpu.VMEM((ZL + 1, NY, 2, OWN, HALF), BF),
            pltpu.VMEM((ZL + 1, NY, 2, OWN, HALF), BF),
            pltpu.VMEM((2, ZH, NX, TILE, HALF), BF),
            pltpu.VMEM((2, ZH, NX, TILE, HALF), BF),
            pltpu.VMEM((2, ZH, TILE, HALF), F32),
            pltpu.VMEM((2, ZH - 1, TILE, HALF), BF),
            pltpu.VMEM((2, ZH - 1, TILE, HALF), BF),
            pltpu.VMEM((2, TILE, 2 * HALF), F32),
            pltpu.VMEM((TILE, 2 * HALF), F32),
            pltpu.VMEM((NY, rows16, 2 * HALF), BF),
            pltpu.VMEM((NY, rows16, 2 * HALF), BF),
            pltpu.VMEM((ZL, rows16, 2 * HALF), F32),
            pltpu.VMEM((NX, rows16, 2 * HALF), F32),
            pltpu.VMEM((ZH, rows16, 2 * HALF), F32),
            pltpu.VMEM((2, NY, rows16, 2 * HALF), BF),
            pltpu.VMEM((N_UNITS, OWN, HALF), BF),
            pltpu.SemaphoreType.DMA((9,)),
            pltpu.SemaphoreType.DMA((2,)),
            pltpu.SemaphoreType.DMA((N_GROUPS,)),
        ],
        compiler_params=pltpu.CompilerParams(
            collective_id=0, has_side_effects=True, vmem_limit_bytes=63 * 2 ** 20
        ),
    )(
        features, weight, tile_values.reshape(NTILES, TILE, TILE),
        tile_rows.transpose(3, 0, 1, 2).reshape(SLOTS, 1, NC), tile_counts.reshape(1, NC), grad_out,
    )


def solution(mesh):
    in_specs = (
        P(("blk", "team"), None),
        P(),
        P("blk", "team", None, None, None, None),
        P("blk", "team", None, None),
        P("blk", "team", None),
        P(("blk", "team"), None),
    )
    out_specs = (P(("blk", "team"), None), P(("blk", "team"), None), P())
    return jax.shard_map(body, mesh=mesh, in_specs=in_specs, out_specs=out_specs, check_vma=False)
```

```python
import math

import jax
import jax.numpy as jnp
from jax import lax
from jax.experimental import pallas as pl
from jax.experimental.pallas import tpu as pltpu
from jax.sharding import PartitionSpec as P

MESH = pl.DeviceIdType.MESH
BF = jnp.bfloat16
F32 = jnp.float32
ZH, NX, ZL, NY = 3, 4, 4, 8
NC = ZH * NX
SLOTS, RT, TILE, HALF, OWN = 6, 16, 128, 128, 32
NTILES = NC * SLOTS
N_GROUPS, N_UNITS = 47, 320


def kernel(
    feat, weight, tiles, rows_in, counts_in, gout_in,
    out, gfeat, gweight,
    tb, tT, wv, gout, rows, counts, inv_v, ridx_v, inv, ridx, xs, acc, pc, rc, s, ry0, rz0, rz1, ry1, t0, t1, gg0, gg1,
    part, fx, own, fs, fz, gw1s, gw1, gw2s, gw2, gw3, gw4, gwa,
    spare, load_sem, send_sem, recv_sem,
):
    blk, team = lax.axis_index("blk"), lax.axis_index("team")
    zh, x = blk // NX, blk % NX
    zl, y, co = team // (2 * NY), (team // 2) % NY, team % 2

    def at(zh_=zh, x_=x, zl_=zl, y_=y, co_=co):
        return (zh_ * NX + x_, (zl_ * NY + y_) * 2 + co_)

    def off(value, d, size):
        return (value + d + size) % size

    other = at(co_=1 - co)
    x_peers = [at(x_=off(x, d, NX)) for d in range(1, NX)]
    y_peers = [at(y_=off(y, d, NY)) for d in range(1, NY)]
    zl_peers = [at(zl_=off(zl, d, ZL)) for d in range(1, ZL)]
    zh_peers = [at(zh_=off(zh, d, ZH)) for d in range(1, ZH)]

    barrier = pltpu.get_barrier_semaphore()
    blk_peers = [(off(blk, d, NC), team) for d in range(1, NC)]
    y_cross = [at(y_=off(y, d, NY), co_=1 - co) for d in range(1, NY)]
    partners = blk_peers + y_peers + y_cross + zl_peers + [other]
    for device in partners:
        pl.semaphore_signal(barrier, inc=1, device_id=device, device_id_type=MESH)

    loads = []

    def load(src, dst):
        copy = pltpu.make_async_copy(src, dst, load_sem.at[len(loads)])
        copy.start()
        loads.append(copy)
        return copy

    load_x = [load(feat.at[:, h * HALF:(h + 1) * HALF], xs.at[h, blk]) for h in range(2)]
    load_index = [load(rows_in, rows), load(counts_in, counts)]
    load_tiles = load(tiles, tb.at[pl.ds(0, NTILES)])
    load_rest = [load(weight, wv), load(gout_in, gout)]

    unit = OWN * HALF * 2
    groups, sent = [], [0, 0, 0]

    def remote(src, dst, group, phase, device):
        return pltpu.make_async_remote_copy(
            src_ref=src, dst_ref=dst, send_sem=send_sem.at[phase], recv_sem=recv_sem.at[group],
            device_id=device, device_id_type=MESH,
        )

    def size(ref):
        return math.prod(ref.shape) * ref.dtype.itemsize // unit

    class Group:
        def __init__(self, phase):
            self.index, self.phase, self.units = len(groups), phase, 0
            groups.append(self)

        def count(self, units):
            self.units += units
            sent[self.phase] += units

        def send(self, src, dst, device):
            remote(src, dst, self.index, self.phase, device).start()
            self.count(size(src))

        def wait(self):
            ref = spare.at[pl.ds(0, self.units)]
            remote(ref, ref, self.index, self.phase, other).wait_recv()

    def send_all(phase, sources, targets, devices):
        group = Group(phase)
        n = len(devices)
        for i in sorted(range(n), key=lambda i: abs(2 * i - n + 1)):
            group.send(sources[i], targets[i], devices[i])
        return group

    def send_same(phase, ref, devices):
        return send_all(phase, [ref] * len(devices), [ref] * len(devices), devices)

    pl.semaphore_wait(barrier, len(partners))

    def send_own(h, devices, phase=0):
        block, target = feat.at[:, h * HALF:(h + 1) * HALF], xs.at[h, blk]
        return send_all(phase, [block] * len(devices), [target] * len(devices), devices)

    def wait_sent(phase):
        ref = spare.at[pl.ds(0, sent[phase])]
        remote(ref, ref, 0, phase, other).wait_send()

    own_z = [[send_own(0, [device], 2) for device in zh_peers]]
    own_x = [send_own(h, x_peers) for h in range(2)]

    tb[NTILES] = jnp.zeros((TILE, TILE), BF)
    for ref in (gg0, gg1):
        ref[ZL] = jnp.zeros((NY, 2, OWN, HALF), BF)

    for copy in load_index:
        copy.wait()
    live = counts[...]
    first_tile = lax.broadcasted_iota(jnp.int32, (1, NC), 1) * SLOTS
    rowof = [jnp.where(k < live, rows[k], RT) for k in range(SLOTS)]
    for k in range(SLOTS):
        ridx_v[k] = jnp.where(rowof[k] == RT, RT, (rowof[k] - zl * (RT // ZL) + RT) & (RT - 1))
    for r in range(RT):
        found = jnp.full((1, NC), NTILES, jnp.int32)
        for k in range(SLOTS):
            found = jnp.where(rowof[k] == r, first_tile + k, found)
        inv_v[r] = found
    load_index = [load(inv_v, inv), load(ridx_v, ridx)]
    wait_sent(2)
    own_z.append([send_own(1, [device]) for device in zh_peers])
    for copy in load_index:
        copy.wait()
    load_tiles.wait()

    def slot(dz, dx):
        return off(zh, dz, ZH) * NX + off(x, dx, NX)

    def forward_group(h, dz, low=0, high=RT // 2):
        cols = [slot(dz, dx) for dx in range(NX)]
        right = jnp.concatenate([xs[h, c] for c in cols], axis=0)

        def step(i, carry):
            left = jnp.concatenate(
                [jnp.concatenate([tb[inv[2 * i + j, 0, c]] for c in cols], axis=1) for j in range(2)], axis=0
            )
            prod = jnp.dot(left, right, preferred_element_type=F32).reshape(4, 2, OWN, HALF)
            zt, yt = i // (NY // 4), pl.ds((i % (NY // 4)) * 4, 4)
            if dz:
                prod += acc[h, zt, yt]
            acc[h, zt, yt] = prod
            if dz == 1:
                pc[h, zt, yt] = prod.astype(BF)
            return carry

        lax.fori_loop(low, high, step, 0)

    def spread(h, d):
        own_z[h][d - 1].wait()
        return send_same(0, xs.at[h, slot(-d, 0)], x_peers)

    def add_partner_core(h, copy):
        copy.wait()
        s[h] = (acc[h, :, :, co] + rc[h].astype(F32)).astype(BF)

    def transpose_body(c, carry):
        for k in range(SLOTS):
            tT[c, :, k * TILE:(k + 1) * TILE] = tb[c * SLOTS + k].T
        return carry

    for copy in load_x:
        copy.wait()
    near = [[None] * ZH, [None] * ZH]
    own_x[0].wait()
    forward_group(0, 0)
    for d in range(1, ZH):
        near[0][ZH - d] = spread(0, d)
    own_x[1].wait()
    forward_group(1, 0)
    for d in range(1, ZH):
        near[1][ZH - d] = spread(1, d)
    core = [Group(0), Group(0)]

    def finish_forward(h):
        for dz in (2, 1):
            near[h][dz].wait()
            if dz == 2:
                forward_group(h, dz)
        for part_ in range(2):
            forward_group(h, 1, part_ * RT // 4, (part_ + 1) * RT // 4)
            rows_ = pl.ds(part_ * ZL // 2, ZL // 2)
            core[h].send(pc.at[h, rows_, :, 1 - co], rc.at[h, rows_], other)

    finish_forward(0)
    add_partner_core(0, core[0])
    y0 = send_all(0, [s.at[0, :, off(y, d, NY)] for d in range(1, NY)], [ry0.at[d] for d in range(1, NY)], y_peers)
    finish_forward(1)
    add_partner_core(1, core[1])
    z1 = send_all(0, [s.at[1, off(zl, d, ZL)] for d in range(1, ZL)], [rz1.at[d] for d in range(1, ZL)], zl_peers)
    lax.fori_loop(0, NC, transpose_body, 0)
    for copy in load_rest:
        copy.wait()

    def add_up(total, ref):
        for d in range(1, ref.shape[0]):
            total += ref[d].astype(F32)
        return total

    z1.wait()
    t1[...] = add_up(s[1, zl].astype(F32), rz1).astype(BF)
    y1 = send_all(0, [t1.at[off(y, d, NY)] for d in range(1, NY)], [ry1.at[d] for d in range(1, NY)], y_peers)
    y0.wait()
    t0[...] = add_up(s[0, :, y].astype(F32), ry0).astype(BF)
    z0 = send_all(0, [t0.at[off(zl, d, ZL)] for d in range(1, ZL)], [rz0.at[d] for d in range(1, ZL)], zl_peers)
    y1.wait()
    ax1 = add_up(t1[y].astype(F32), ry1)
    z0.wait()
    ax0 = add_up(t0[zl].astype(F32), rz0)

    ax = jnp.concatenate([ax0, ax1], axis=1)
    high = ax.astype(BF)
    low = (ax - high.astype(F32)).astype(BF)
    w = wv[...]
    pre = jnp.dot(high, w, preferred_element_type=F32) + jnp.dot(low, w, preferred_element_type=F32)
    sig = jax.nn.sigmoid(pre)
    grad = (gout[...].astype(F32) * sig * (1.0 + pre * (1.0 - sig))).astype(BF)
    back = lax.dot_general(grad, w, (((1,), (1,)), ((), ())), preferred_element_type=F32).astype(BF)
    gg0[0, y, co] = back[:, :HALF]
    gg1[0, y, co] = back[:, HALF:]

    def to_zl(ref, place):
        group = Group(1)
        for d in range(1, ZL):
            group.send(ref.at[(0,) + place], ref.at[(ZL - d,) + place], zl_peers[d - 1])
        return group

    a0 = to_zl(gg0, (y, co))
    a1 = send_same(1, gg1.at[0, y, co], y_peers)
    b0 = [send_same(1, gg0.at[0, y, co], [device]) for device in y_peers]
    out[...] = (pre * sig).astype(BF)

    gw1s[...] = lax.dot_general(
        jnp.concatenate([high, low], axis=0), jnp.concatenate([grad, grad], axis=0),
        (((0,), (0,)), ((), ())), preferred_element_type=F32,
    ).reshape(2, TILE, 2 * HALF)
    g1 = send_all(1, [gw1s.at[1 - co]], [gw1], [other])
    g1.wait()
    gw2s[...] = (gw1s[co] + gw1[...]).reshape(NY, OWN // 2, 2 * HALF).astype(BF)
    g2 = send_all(1, [gw2s.at[off(y, d, NY)] for d in range(1, NY)], [gw2.at[d] for d in range(1, NY)], y_peers)

    a0.wait()
    line = gg0.at[pl.ds(1, ZL - 1), y, co]
    by_distance = sorted(range(1, NY), key=lambda d: -min(d, NY - d))
    for d in by_distance:
        b0[d - 1].send(line, line, y_peers[d - 1])
    line = gg0.at[pl.ds(0, ZL), y, co]
    c0 = send_same(1, line, [other])
    a1.wait()
    line = gg1.at[0, :, co]
    b1 = [send_all(1, [line], [gg1.at[ZL - d, :, co]], [zl_peers[d - 1]]) for d in range(1, ZL)]
    c1 = send_same(1, line, [other])
    g2.wait()
    gw3[zl] = add_up(gw2s[y].astype(F32), gw2)
    g3 = send_same(1, gw3.at[zl], zl_peers)
    for d in range(1, ZL):
        b1[d - 1].wait()
        line = gg1.at[ZL - d, :, co]
        c1.send(line, line, other)
    for d in by_distance[::-1]:
        b0[d - 1].wait()
        line = gg0.at[pl.ds(0, ZL), off(y, -d, NY), co]
        c0.send(line, line, other)
    g3.wait()
    gw4[blk] = ((gw3[0] + gw3[1]) + (gw3[2] + gw3[3])).astype(BF)
    g4 = send_same(1, gw4.at[blk], blk_peers)

    def back_term(h, dz, dx):
        ref = (gg0, gg1)[h]
        c = slot(dz, dx)
        picks = []
        for k in range(SLOTS):
            r = ridx[k, 0, c]
            picks.append(ref[r >> 2, pl.ds((r & 3) * 2, 2)].reshape(TILE, HALF))
        return jnp.dot(tT[c], jnp.concatenate(picks, axis=0), preferred_element_type=F32)

    sx = {}

    def products(h, low, count):
        base = len(groups)
        for dz in range(low, low + count):
            sx[h, dz] = Group(1)
            sx[h, dz].count((NX - 1) * size(part.at[h, dz, 0]))

        def step(i, carry):
            dz, j = low + i // (NX - 1), i % (NX - 1)
            dx = 2 - j + 3 * (j // 2)
            part[h, dz, dx] = back_term(h, dz, dx).astype(BF)
            remote(part.at[h, dz, dx], fx.at[h, dz, dx], base + i // (NX - 1), 1, at(x_=off(x, dx, NX))).start()
            return carry

        lax.fori_loop(0, count * (NX - 1), step, 0)

    def own_products(h):
        def step(dz, carry):
            own[h, dz] = back_term(h, dz, 0)
            return carry

        lax.fori_loop(0, ZH, step, 0)

    def total_over_x(h, dz):
        sx[h, dz].wait()
        return add_up(own[h, dz], fx.at[h, dz])

    sz = {}

    def to_z(h, dz):
        fs[h, dz - 1] = total_over_x(h, dz).astype(BF)
        sz[h, dz] = send_all(1, [fs.at[h, dz - 1]], [fz.at[h, dz - 1]], [zh_peers[dz - 1]])

    def finish(h):
        term = own[h, 0]
        for dz in range(1, ZH):
            sz[h, dz].wait()
            term += fz[h, dz - 1].astype(F32)
        gfeat[:, h * HALF:(h + 1) * HALF] = term.astype(BF)

    c1.wait()
    products(1, 1, 2)
    c0.wait()
    products(0, 1, 2)
    own_products(1)
    for dz in range(1, ZH):
        to_z(1, dz)
    own_products(0)
    for dz in range(1, ZH):
        to_z(0, dz)
    g4.wait()
    sub = gw4[0].astype(F32)
    for c in range(1, NC):
        sub += gw4[c].astype(F32)
    gwa[co, y] = sub.astype(BF)
    g5 = send_same(1, gwa.at[co, y], y_peers + y_cross + [other])
    products(1, 0, 1)
    products(0, 0, 1)
    for h in (1, 0):
        own[h, 0] = total_over_x(h, 0)
    finish(1)
    finish(0)
    g5.wait()
    gweight[...] = gwa[...].reshape(2 * HALF, 2 * HALF).astype(F32)
    for phase in range(2):
        wait_sent(phase)


def body(features, weight, tile_values, tile_rows, tile_counts, grad_out):
    vmem = pl.BlockSpec(memory_space=pltpu.VMEM)
    hbm = pl.BlockSpec(memory_space=pltpu.HBM)
    rows16 = OWN // 2
    return pl.pallas_call(
        kernel,
        out_shape=(
            pltpu.VMEM(grad_out.shape, BF),
            pltpu.VMEM(features.shape, BF),
            pltpu.VMEM(weight.shape, F32),
        ),
        in_specs=[hbm] * 6,
        out_specs=(vmem, vmem, vmem),
        scratch_shapes=[
            pltpu.VMEM((NTILES + 1, TILE, TILE), BF),
            pltpu.VMEM((NC, TILE, SLOTS * TILE), BF),
            pltpu.VMEM(weight.shape, BF),
            pltpu.VMEM(grad_out.shape, BF),
            pltpu.VMEM((SLOTS, 1, NC), jnp.int32),
            pltpu.VMEM((1, NC), jnp.int32),
            pltpu.VMEM((RT, 1, NC), jnp.int32),
            pltpu.VMEM((SLOTS, 1, NC), jnp.int32),
            pltpu.SMEM((RT, 1, NC), jnp.int32),
            pltpu.SMEM((SLOTS, 1, NC), jnp.int32),
            pltpu.VMEM((2, NC, TILE, HALF), BF),
            pltpu.VMEM((2, ZL, NY, 2, OWN, HALF), F32),
            pltpu.VMEM((2, ZL, NY, 2, OWN, HALF), BF),
            pltpu.VMEM((2, ZL, NY, OWN, HALF), BF),
            pltpu.VMEM((2, ZL, NY, OWN, HALF), BF),
            pltpu.VMEM((NY, ZL, OWN, HALF), BF),
            pltpu.VMEM((ZL, OWN, HALF), BF),
            pltpu.VMEM((ZL, NY, OWN, HALF), BF),
            pltpu.VMEM((NY, OWN, HALF), BF),
            pltpu.VMEM((ZL, OWN, HALF), BF),
            pltpu.VMEM((NY, OWN, HALF), BF),
            pltpu.VMEM((ZL + 1, NY, 2, OWN, HALF), BF),
            pltpu.VMEM((ZL + 1, NY, 2, OWN, HALF), BF),
            pltpu.VMEM((2, ZH, NX, TILE, HALF), BF),
            pltpu.VMEM((2, ZH, NX, TILE, HALF), BF),
            pltpu.VMEM((2, ZH, TILE, HALF), F32),
            pltpu.VMEM((2, ZH - 1, TILE, HALF), BF),
            pltpu.VMEM((2, ZH - 1, TILE, HALF), BF),
            pltpu.VMEM((2, TILE, 2 * HALF), F32),
            pltpu.VMEM((TILE, 2 * HALF), F32),
            pltpu.VMEM((NY, rows16, 2 * HALF), BF),
            pltpu.VMEM((NY, rows16, 2 * HALF), BF),
            pltpu.VMEM((ZL, rows16, 2 * HALF), F32),
            pltpu.VMEM((NC, rows16, 2 * HALF), BF),
            pltpu.VMEM((2, NY, rows16, 2 * HALF), BF),
            pltpu.VMEM((N_UNITS, OWN, HALF), BF),
            pltpu.SemaphoreType.DMA((9,)),
            pltpu.SemaphoreType.DMA((3,)),
            pltpu.SemaphoreType.DMA((N_GROUPS,)),
        ],
        compiler_params=pltpu.CompilerParams(
            collective_id=0, has_side_effects=True, vmem_limit_bytes=58 * 2 ** 20
        ),
    )(
        features, weight, tile_values.reshape(NTILES, TILE, TILE),
        tile_rows.transpose(3, 0, 1, 2).reshape(SLOTS, 1, NC), tile_counts.reshape(1, NC), grad_out,
    )


def solution(mesh):
    in_specs = (
        P(("blk", "team"), None),
        P(),
        P("blk", "team", None, None, None, None),
        P("blk", "team", None, None),
        P("blk", "team", None),
        P(("blk", "team"), None),
    )
    out_specs = (P(("blk", "team"), None), P(("blk", "team"), None), P())
    return jax.shard_map(body, mesh=mesh, in_specs=in_specs, out_specs=out_specs, check_vma=False)
```

```python
import math

import jax
import jax.numpy as jnp
from jax import lax
from jax.experimental import pallas as pl
from jax.experimental.pallas import tpu as pltpu
from jax.sharding import PartitionSpec as P

MESH = pl.DeviceIdType.MESH
BF = jnp.bfloat16
F32 = jnp.float32
ZH, NX, ZL, NY = 3, 4, 4, 8
NC = ZH * NX
SLOTS, RT, TILE, HALF, OWN = 6, 16, 128, 128, 32
NTILES = NC * SLOTS
N_GROUPS, N_UNITS = 47, 320


def kernel(
    feat, weight, tiles, rows_in, counts_in, gout_in,
    out, gfeat, gweight,
    tb, tT, wv, gout, rows, counts, inv_v, ridx_v, inv, ridx, xs, acc, pc, rc, s, ry0, rz0, rz1, ry1, t0, t1, gg0, gg1,
    part, fx, own, fs, fz, gw1s, gw1, gw2s, gw2, gw3, gw4, gwa,
    spare, load_sem, send_sem, recv_sem,
):
    blk, team = lax.axis_index("blk"), lax.axis_index("team")
    zh, x = blk // NX, blk % NX
    zl, y, co = team // (2 * NY), (team // 2) % NY, team % 2

    def at(zh_=zh, x_=x, zl_=zl, y_=y, co_=co):
        return (zh_ * NX + x_, (zl_ * NY + y_) * 2 + co_)

    def off(value, d, size):
        return (value + d + size) % size

    other = at(co_=1 - co)
    x_peers = [at(x_=off(x, d, NX)) for d in range(1, NX)]
    y_peers = [at(y_=off(y, d, NY)) for d in range(1, NY)]
    zl_peers = [at(zl_=off(zl, d, ZL)) for d in range(1, ZL)]
    zh_peers = [at(zh_=off(zh, d, ZH)) for d in range(1, ZH)]

    barrier = pltpu.get_barrier_semaphore()
    blk_peers = [(off(blk, d, NC), team) for d in range(1, NC)]
    y_cross = [at(y_=off(y, d, NY), co_=1 - co) for d in range(1, NY)]
    partners = blk_peers + y_peers + y_cross + zl_peers + [other]
    for device in partners:
        pl.semaphore_signal(barrier, inc=1, device_id=device, device_id_type=MESH)

    loads = []

    def load(src, dst):
        copy = pltpu.make_async_copy(src, dst, load_sem.at[len(loads)])
        copy.start()
        loads.append(copy)
        return copy

    load_x = [load(feat.at[:, h * HALF:(h + 1) * HALF], xs.at[h, blk]) for h in range(2)]
    load_index = [load(rows_in, rows), load(counts_in, counts)]
    load_tiles = load(tiles, tb.at[pl.ds(0, NTILES)])
    load_rest = [load(weight, wv), load(gout_in, gout)]

    unit = OWN * HALF * 2
    groups, sent = [], [0, 0, 0]

    def remote(src, dst, group, phase, device):
        return pltpu.make_async_remote_copy(
            src_ref=src, dst_ref=dst, send_sem=send_sem.at[phase], recv_sem=recv_sem.at[group],
            device_id=device, device_id_type=MESH,
        )

    def size(ref):
        return math.prod(ref.shape) * ref.dtype.itemsize // unit

    class Group:
        def __init__(self, phase):
            self.index, self.phase, self.units = len(groups), phase, 0
            groups.append(self)

        def count(self, units):
            self.units += units
            sent[self.phase] += units

        def send(self, src, dst, device):
            remote(src, dst, self.index, self.phase, device).start()
            self.count(size(src))

        def wait(self):
            ref = spare.at[pl.ds(0, self.units)]
            remote(ref, ref, self.index, self.phase, other).wait_recv()

    def send_all(phase, sources, targets, devices):
        group = Group(phase)
        n = len(devices)
        for i in sorted(range(n), key=lambda i: abs(2 * i - n + 1)):
            group.send(sources[i], targets[i], devices[i])
        return group

    def send_same(phase, ref, devices):
        return send_all(phase, [ref] * len(devices), [ref] * len(devices), devices)

    pl.semaphore_wait(barrier, len(partners))

    def send_own(h, devices, phase=0):
        block, target = feat.at[:, h * HALF:(h + 1) * HALF], xs.at[h, blk]
        return send_all(phase, [block] * len(devices), [target] * len(devices), devices)

    def wait_sent(phase):
        ref = spare.at[pl.ds(0, sent[phase])]
        remote(ref, ref, 0, phase, other).wait_send()

    own_z = [[send_own(0, [device], 2) for device in zh_peers]]
    own_x = [send_own(h, x_peers) for h in range(2)]

    tb[NTILES] = jnp.zeros((TILE, TILE), BF)
    for ref in (gg0, gg1):
        ref[ZL] = jnp.zeros((NY, 2, OWN, HALF), BF)

    for copy in load_index:
        copy.wait()
    live = counts[...]
    first_tile = lax.broadcasted_iota(jnp.int32, (1, NC), 1) * SLOTS
    rowof = [jnp.where(k < live, rows[k], RT) for k in range(SLOTS)]
    for k in range(SLOTS):
        ridx_v[k] = jnp.where(rowof[k] == RT, RT, (rowof[k] - zl * (RT // ZL) + RT) & (RT - 1))
    for r in range(RT):
        found = jnp.full((1, NC), NTILES, jnp.int32)
        for k in range(SLOTS):
            found = jnp.where(rowof[k] == r, first_tile + k, found)
        inv_v[r] = found
    load_index = [load(inv_v, inv), load(ridx_v, ridx)]
    wait_sent(2)
    own_z.append([send_own(1, [device]) for device in zh_peers])
    for copy in load_index:
        copy.wait()
    load_tiles.wait()

    def slot(dz, dx):
        return off(zh, dz, ZH) * NX + off(x, dx, NX)

    def forward_group(h, groups_, low=0, high=RT // 2):
        cols = [slot(dz, dx) for dz in groups_ for dx in range(NX)]
        right = jnp.concatenate([xs[h, c] for c in cols], axis=0)

        def step(i, carry):
            left = jnp.concatenate(
                [jnp.concatenate([tb[inv[2 * i + j, 0, c]] for c in cols], axis=1) for j in range(2)], axis=0
            )
            prod = jnp.dot(left, right, preferred_element_type=F32).reshape(4, 2, OWN, HALF)
            zt, yt = i // (NY // 4), pl.ds((i % (NY // 4)) * 4, 4)
            if 0 not in groups_:
                prod += acc[h, zt, yt]
            acc[h, zt, yt] = prod
            if 1 in groups_:
                pc[h, zt, yt] = prod.astype(BF)
            return carry

        lax.fori_loop(low, high, step, 0)

    def spread(h, d):
        own_z[h][d - 1].wait()
        return send_same(0, xs.at[h, slot(-d, 0)], x_peers)

    def add_partner_core(h, copy):
        copy.wait()
        s[h] = (acc[h, :, :, co] + rc[h].astype(F32)).astype(BF)

    def transpose_body(c, carry):
        for k in range(SLOTS):
            tT[c, :, k * TILE:(k + 1) * TILE] = tb[c * SLOTS + k].T
        return carry

    for copy in load_x:
        copy.wait()
    near = [[None] * ZH, [None] * ZH]
    own_x[0].wait()
    forward_group(0, (0,))
    for d in range(1, ZH):
        near[0][ZH - d] = spread(0, d)
    own_x[1].wait()
    forward_group(1, (0,))
    for d in range(1, ZH):
        near[1][ZH - d] = spread(1, d)
    core = [Group(0), Group(0)]

    def last_group(h):
        near[h][2].wait()
        near[h][1].wait()
        for part_ in range(2):
            forward_group(h, (2, 1), part_ * RT // 4, (part_ + 1) * RT // 4)
            rows_ = pl.ds(part_ * ZL // 2, ZL // 2)
            core[h].send(pc.at[h, rows_, :, 1 - co], rc.at[h, rows_], other)

    last_group(0)
    add_partner_core(0, core[0])
    y0 = send_all(0, [s.at[0, :, off(y, d, NY)] for d in range(1, NY)], [ry0.at[d] for d in range(1, NY)], y_peers)
    last_group(1)
    add_partner_core(1, core[1])
    z1 = send_all(0, [s.at[1, off(zl, d, ZL)] for d in range(1, ZL)], [rz1.at[d] for d in range(1, ZL)], zl_peers)
    lax.fori_loop(0, NC, transpose_body, 0)
    for copy in load_rest:
        copy.wait()

    def add_up(total, ref):
        for d in range(1, ref.shape[0]):
            total += ref[d].astype(F32)
        return total

    z1.wait()
    t1[...] = add_up(s[1, zl].astype(F32), rz1).astype(BF)
    y1 = send_all(0, [t1.at[off(y, d, NY)] for d in range(1, NY)], [ry1.at[d] for d in range(1, NY)], y_peers)
    y0.wait()
    t0[...] = add_up(s[0, :, y].astype(F32), ry0).astype(BF)
    z0 = send_all(0, [t0.at[off(zl, d, ZL)] for d in range(1, ZL)], [rz0.at[d] for d in range(1, ZL)], zl_peers)
    y1.wait()
    ax1 = add_up(t1[y].astype(F32), ry1)
    z0.wait()
    ax0 = add_up(t0[zl].astype(F32), rz0)

    ax = jnp.concatenate([ax0, ax1], axis=1)
    high = ax.astype(BF)
    low = (ax - high.astype(F32)).astype(BF)
    w = wv[...]
    pre = jnp.dot(high, w, preferred_element_type=F32) + jnp.dot(low, w, preferred_element_type=F32)
    sig = jax.nn.sigmoid(pre)
    grad = (gout[...].astype(F32) * sig * (1.0 + pre * (1.0 - sig))).astype(BF)
    back = lax.dot_general(grad, w, (((1,), (1,)), ((), ())), preferred_element_type=F32).astype(BF)
    gg0[0, y, co] = back[:, :HALF]
    gg1[0, y, co] = back[:, HALF:]

    def to_zl(ref, place):
        group = Group(1)
        for d in range(1, ZL):
            group.send(ref.at[(0,) + place], ref.at[(ZL - d,) + place], zl_peers[d - 1])
        return group

    a0 = to_zl(gg0, (y, co))
    a1 = send_same(1, gg1.at[0, y, co], y_peers)
    b0 = [send_same(1, gg0.at[0, y, co], [device]) for device in y_peers]
    out[...] = (pre * sig).astype(BF)

    gw1s[...] = lax.dot_general(
        jnp.concatenate([high, low], axis=0), jnp.concatenate([grad, grad], axis=0),
        (((0,), (0,)), ((), ())), preferred_element_type=F32,
    ).reshape(2, TILE, 2 * HALF)
    g1 = send_all(1, [gw1s.at[1 - co]], [gw1], [other])
    g1.wait()
    gw2s[...] = (gw1s[co] + gw1[...]).reshape(NY, OWN // 2, 2 * HALF).astype(BF)
    g2 = send_all(1, [gw2s.at[off(y, d, NY)] for d in range(1, NY)], [gw2.at[d] for d in range(1, NY)], y_peers)

    a0.wait()
    line = gg0.at[pl.ds(1, ZL - 1), y, co]
    by_distance = sorted(range(1, NY), key=lambda d: -min(d, NY - d))
    for d in by_distance:
        b0[d - 1].send(line, line, y_peers[d - 1])
    line = gg0.at[pl.ds(0, ZL), y, co]
    c0 = send_same(1, line, [other])
    a1.wait()
    line = gg1.at[0, :, co]
    b1 = [send_all(1, [line], [gg1.at[ZL - d, :, co]], [zl_peers[d - 1]]) for d in range(1, ZL)]
    c1 = send_same(1, line, [other])
    g2.wait()
    gw3[zl] = add_up(gw2s[y].astype(F32), gw2)
    g3 = send_same(1, gw3.at[zl], zl_peers)
    for d in range(1, ZL):
        b1[d - 1].wait()
        line = gg1.at[ZL - d, :, co]
        c1.send(line, line, other)
    for d in by_distance[::-1]:
        b0[d - 1].wait()
        line = gg0.at[pl.ds(0, ZL), off(y, -d, NY), co]
        c0.send(line, line, other)
    g3.wait()
    gw4[blk] = ((gw3[0] + gw3[1]) + (gw3[2] + gw3[3])).astype(BF)
    g4 = send_same(1, gw4.at[blk], blk_peers)

    def back_term(h, dz, dx):
        ref = (gg0, gg1)[h]
        c = slot(dz, dx)
        picks = []
        for k in range(SLOTS):
            r = ridx[k, 0, c]
            picks.append(ref[r >> 2, pl.ds((r & 3) * 2, 2)].reshape(TILE, HALF))
        return jnp.dot(tT[c], jnp.concatenate(picks, axis=0), preferred_element_type=F32)

    sx = {}

    def products(h, low, count):
        base = len(groups)
        for dz in range(low, low + count):
            sx[h, dz] = Group(1)
            sx[h, dz].count((NX - 1) * size(part.at[h, dz, 0]))

        def step(i, carry):
            dz, j = low + i // (NX - 1), i % (NX - 1)
            dx = 2 - j + 3 * (j // 2)
            part[h, dz, dx] = back_term(h, dz, dx).astype(BF)
            remote(part.at[h, dz, dx], fx.at[h, dz, dx], base + i // (NX - 1), 1, at(x_=off(x, dx, NX))).start()
            return carry

        lax.fori_loop(0, count * (NX - 1), step, 0)

    def own_products(h):
        def step(dz, carry):
            own[h, dz] = back_term(h, dz, 0)
            return carry

        lax.fori_loop(0, ZH, step, 0)

    def total_over_x(h, dz):
        sx[h, dz].wait()
        return add_up(own[h, dz], fx.at[h, dz])

    sz = {}

    def to_z(h, dz):
        fs[h, dz - 1] = total_over_x(h, dz).astype(BF)
        sz[h, dz] = send_all(1, [fs.at[h, dz - 1]], [fz.at[h, dz - 1]], [zh_peers[dz - 1]])

    def finish(h):
        term = own[h, 0]
        for dz in range(1, ZH):
            sz[h, dz].wait()
            term += fz[h, dz - 1].astype(F32)
        gfeat[:, h * HALF:(h + 1) * HALF] = term.astype(BF)

    c1.wait()
    products(1, 1, 2)
    c0.wait()
    products(0, 1, 2)
    own_products(1)
    for dz in range(1, ZH):
        to_z(1, dz)
    own_products(0)
    for dz in range(1, ZH):
        to_z(0, dz)
    g4.wait()
    sub = gw4[0].astype(F32)
    for c in range(1, NC):
        sub += gw4[c].astype(F32)
    gwa[co, y] = sub.astype(BF)
    g5 = send_same(1, gwa.at[co, y], y_peers + y_cross + [other])
    products(1, 0, 1)
    products(0, 0, 1)
    for h in (1, 0):
        own[h, 0] = total_over_x(h, 0)
    finish(1)
    finish(0)
    g5.wait()
    gweight[...] = gwa[...].reshape(2 * HALF, 2 * HALF).astype(F32)
    for phase in range(2):
        wait_sent(phase)


def body(features, weight, tile_values, tile_rows, tile_counts, grad_out):
    vmem = pl.BlockSpec(memory_space=pltpu.VMEM)
    hbm = pl.BlockSpec(memory_space=pltpu.HBM)
    rows16 = OWN // 2
    return pl.pallas_call(
        kernel,
        out_shape=(
            pltpu.VMEM(grad_out.shape, BF),
            pltpu.VMEM(features.shape, BF),
            pltpu.VMEM(weight.shape, F32),
        ),
        in_specs=[hbm] * 6,
        out_specs=(vmem, vmem, vmem),
        scratch_shapes=[
            pltpu.VMEM((NTILES + 1, TILE, TILE), BF),
            pltpu.VMEM((NC, TILE, SLOTS * TILE), BF),
            pltpu.VMEM(weight.shape, BF),
            pltpu.VMEM(grad_out.shape, BF),
            pltpu.VMEM((SLOTS, 1, NC), jnp.int32),
            pltpu.VMEM((1, NC), jnp.int32),
            pltpu.VMEM((RT, 1, NC), jnp.int32),
            pltpu.VMEM((SLOTS, 1, NC), jnp.int32),
            pltpu.SMEM((RT, 1, NC), jnp.int32),
            pltpu.SMEM((SLOTS, 1, NC), jnp.int32),
            pltpu.VMEM((2, NC, TILE, HALF), BF),
            pltpu.VMEM((2, ZL, NY, 2, OWN, HALF), F32),
            pltpu.VMEM((2, ZL, NY, 2, OWN, HALF), BF),
            pltpu.VMEM((2, ZL, NY, OWN, HALF), BF),
            pltpu.VMEM((2, ZL, NY, OWN, HALF), BF),
            pltpu.VMEM((NY, ZL, OWN, HALF), BF),
            pltpu.VMEM((ZL, OWN, HALF), BF),
            pltpu.VMEM((ZL, NY, OWN, HALF), BF),
            pltpu.VMEM((NY, OWN, HALF), BF),
            pltpu.VMEM((ZL, OWN, HALF), BF),
            pltpu.VMEM((NY, OWN, HALF), BF),
            pltpu.VMEM((ZL + 1, NY, 2, OWN, HALF), BF),
            pltpu.VMEM((ZL + 1, NY, 2, OWN, HALF), BF),
            pltpu.VMEM((2, ZH, NX, TILE, HALF), BF),
            pltpu.VMEM((2, ZH, NX, TILE, HALF), BF),
            pltpu.VMEM((2, ZH, TILE, HALF), F32),
            pltpu.VMEM((2, ZH - 1, TILE, HALF), BF),
            pltpu.VMEM((2, ZH - 1, TILE, HALF), BF),
            pltpu.VMEM((2, TILE, 2 * HALF), F32),
            pltpu.VMEM((TILE, 2 * HALF), F32),
            pltpu.VMEM((NY, rows16, 2 * HALF), BF),
            pltpu.VMEM((NY, rows16, 2 * HALF), BF),
            pltpu.VMEM((ZL, rows16, 2 * HALF), F32),
            pltpu.VMEM((NC, rows16, 2 * HALF), BF),
            pltpu.VMEM((2, NY, rows16, 2 * HALF), BF),
            pltpu.VMEM((N_UNITS, OWN, HALF), BF),
            pltpu.SemaphoreType.DMA((9,)),
            pltpu.SemaphoreType.DMA((3,)),
            pltpu.SemaphoreType.DMA((N_GROUPS,)),
        ],
        compiler_params=pltpu.CompilerParams(
            collective_id=0, has_side_effects=True, vmem_limit_bytes=58 * 2 ** 20
        ),
    )(
        features, weight, tile_values.reshape(NTILES, TILE, TILE),
        tile_rows.transpose(3, 0, 1, 2).reshape(SLOTS, 1, NC), tile_counts.reshape(1, NC), grad_out,
    )


def solution(mesh):
    in_specs = (
        P(("blk", "team"), None),
        P(),
        P("blk", "team", None, None, None, None),
        P("blk", "team", None, None),
        P("blk", "team", None),
        P(("blk", "team"), None),
    )
    out_specs = (P(("blk", "team"), None), P(("blk", "team"), None), P())
    return jax.shard_map(body, mesh=mesh, in_specs=in_specs, out_specs=out_specs, check_vma=False)
```
